32 devices in a mesh: event: 2 (over core), dom: 16 (over z, y, x).
Axes of the slice: x: 2, y: 2, z: 4, core: 2. Of those that a mesh axis runs over, the one named last changes fastest.
Arguments:
- kernels: bfloat16 [4, 16, 64, 125, 128], P('event', 'dom'), may hold values from -12 to 12
- counts: int32 [4, 16, 64, 128], P('event', 'dom'), may hold values from 0 to 3
- volume: bfloat16 [16, 64, 128], P('dom', 'event'), may hold values from 0.29882812 to 3
- tables: bfloat16 [32, 128, 128], replicated, may hold values from 0.049804688 to 1
- pair_offset: int32 [16, 2, 32, 16], P('dom', 'event'), may hold values from 0 to 64, as said below
- pair_table: int32 [16, 2, 32, 16], P('dom', 'event'), may hold values from 0 to 31
Outputs:
- smoothed: bfloat16 [16, 64, 125, 128], P('dom', 'event')
The draws below stay inside these ranges and needn't reach their ends.
Inputs may be any that keep to these rules, and one draw needn't show every extreme that they name: `pair_offset`: for each block of a device the 16 offsets are distinct and the first is 32.
All inputs are finite; a program needn't handle non-finite values.
Results may differ from the reference program's by a relative error of at most 0.0075.
Values may be sent and summed in bfloat16 or wider, within the bound.
A program may use at most 64 MiB of HBM per device.

```python
import math
import jax
import jax.numpy as jnp
from jax import lax

G = 125
BLK = 128
EV_DEV = 2
OWN_BLK = 32
PB = 16
TABLES = 32
EVENTS = 4
NSUB = 2
PART_BLK = 64
NPART = 16
N_EVENT = 2


def draw_kernels(key, part):
    first, second = jax.random.split(key)
    shape = (EVENTS, NPART, PART_BLK, G, BLK)
    level_shape = (EVENTS, NPART, PART_BLK, G, 1)
    rough = jax.random.normal(first, shape, jnp.float32)
    level = jax.random.normal(second, level_shape, jnp.float32)
    return jnp.clip(rough + level, -12.0, 12.0).astype(jnp.bfloat16)


def draw_pair_offset(key, part):
    window = 2 * OWN_BLK + 1
    scores = jax.random.randint(key, (NPART, NSUB, OWN_BLK, window), 0, 2 ** 20) * 1024
    columns = jnp.arange(window, dtype=jnp.int32)
    scores = scores + columns
    scores = jnp.where(columns == OWN_BLK, -1, scores)
    order = jnp.argsort(scores, axis=-1)
    return order[..., :PB].astype(jnp.int32)


def touch_ends(drawn, rng, low, high):
    longest = drawn.shape.index(max(drawn.shape))
    spots = []
    for shift in (0, 1):
        where = [jax.random.randint(jax.random.fold_in(rng, axis), (), 0, length) for axis, length in enumerate(drawn.shape)]
        where[longest] = (where[longest] + shift) % drawn.shape[longest]
        spots.append(tuple(where))
    return drawn.at[spots[0]].set(low).at[spots[1]].set(high)


def level_of(stream_key, dims, cuts, smallest, top_value):
    loudness = 1.0
    for dim, blocks in cuts:
        heights = jax.random.uniform(jax.random.fold_in(jax.random.fold_in(stream_key, 6), dim), (blocks,), jnp.float32, smallest / len(cuts), top_value / len(cuts))
        loudness = loudness * jnp.repeat(jnp.exp(heights), dims[dim] // blocks).reshape((-1,) + (1,) * (len(dims) - 1 - dim))
    return loudness


def setup_inputs(seed: int = 0) -> dict:
    key_list = jax.random.split(jax.random.key(seed), 7)
    kernels = draw_kernels(jax.random.fold_in(key_list[6], 71), 0)
    counts = touch_ends(jax.random.randint(key_list[1], (EVENTS, NPART, PART_BLK, BLK), 0, 4), jax.random.fold_in(key_list[1], 1), 0, 3).astype(jnp.int32)
    volume = jnp.clip(jnp.exp(math.log(3.0) - 2.306499 * jax.random.uniform(key_list[2], (NPART, PART_BLK, BLK), jnp.float32) ** level_of(key_list[2], (NPART, PART_BLK, BLK), ((0, 16), (1, 2)), -0.2, 0.2)), 0.29882812, 3.0).astype(jnp.bfloat16)
    tables = jnp.clip(jax.random.uniform(key_list[3], (TABLES, BLK, BLK), jnp.float32, 0.049804688, 1.0), 0.049804688, 1.0).astype(jnp.bfloat16)
    pair_offset = draw_pair_offset(jax.random.fold_in(key_list[6], 71), 0)
    pair_table = touch_ends(jax.random.randint(key_list[5], (NPART, NSUB, OWN_BLK, PB), 0, TABLES), jax.random.fold_in(key_list[5], 1), 0, TABLES - 1).astype(jnp.int32)
    return dict(kernels=kernels, counts=counts, volume=volume, tables=tables, pair_offset=pair_offset, pair_table=pair_table)


def add_terms(extended, targets, contrib):
    return extended.at[targets].add(contrib)

def contributions(source, offsets, table_ids, tables):
    extended = jnp.zeros((NSUB, 3 * OWN_BLK, G + 1, BLK), jnp.float32)
    places = jnp.arange(OWN_BLK, dtype=jnp.int32)
    for which in range(PB):
        matrices = tables[table_ids[:, :, which]].astype(jnp.float32)
        contrib = jnp.einsum('sbgc,sbct->sbgt', source, matrices, precision=lax.Precision.HIGHEST)
        targets = (places[None, :] + offsets[:, :, which]).astype(jnp.int32)
        extended = jax.vmap(add_terms)(extended, targets, contrib)
    return extended

def reference(kernels, counts, volume, tables, pair_offset, pair_table):

    def per_partition(index):
        block = lax.dynamic_index_in_dim(kernels, index, 1, keepdims=False)
        grouped = block.reshape(N_EVENT, EV_DEV, PART_BLK, G, BLK)
        partial_value = lax.optimization_barrier(jnp.sum(grouped.astype(jnp.float32), axis=1)).astype(jnp.bfloat16)
        summed = lax.optimization_barrier(jnp.sum(partial_value.astype(jnp.float32), axis=0))
        count_part = lax.dynamic_index_in_dim(counts, index, 1, keepdims=False)
        hits = lax.optimization_barrier(jnp.sum(count_part.astype(jnp.float32), axis=0))
        vol_part = lax.dynamic_index_in_dim(volume, index, 0, keepdims=False)
        weighted = (summed * vol_part.astype(jnp.float32)[:, None, :] / jnp.sqrt(1.0 + hits)[:, None, :]).astype(jnp.bfloat16)
        source = jnp.concatenate([weighted, vol_part[:, None, :]], axis=1).astype(jnp.float32)
        source = source.reshape(NSUB, OWN_BLK, G + 1, BLK)
        offsets = lax.dynamic_index_in_dim(pair_offset, index, 0, keepdims=False)
        table_ids = lax.dynamic_index_in_dim(pair_table, index, 0, keepdims=False)
        return contributions(source, offsets, table_ids, tables)
    extended = lax.map(per_partition, jnp.arange(NPART, dtype=jnp.int32))
    middle = extended[:, :, OWN_BLK:2 * OWN_BLK]
    empty = jnp.zeros((1, NSUB, OWN_BLK, G + 1, BLK), jnp.float32)
    from_next = jnp.concatenate([extended[1:, :, :OWN_BLK], empty], axis=0)
    from_prev = jnp.concatenate([empty, extended[:-1, :, 2 * OWN_BLK:]], axis=0)
    accumulated = (middle + from_next + from_prev).reshape(NPART, PART_BLK, G + 1, BLK)
    result = accumulated[:, :, :G, :] / accumulated[:, :, G:G + 1, :]
    return result.astype(jnp.bfloat16)
```

```python
import functools

import jax
import jax.numpy as jnp
from jax import lax
from jax.experimental import pallas as pl
from jax.experimental.pallas import tpu as pltpu
from jax.sharding import PartitionSpec as P

CHUNK = 4
MESH = pl.DeviceIdType.MESH


def kernel(
    sizes,
    kernels, counts, volume, tables, index_smem, index_vmem, out,
    kbuf, part_out, part_in, count_out, count_in, scale, vol, stage,
    source, mate, far, tab, acc, index_mate, index_far, index_mate_s, index_far_s,
    ksem, tsem, csem, xsem, isem, msem, fsem,
):
    n = sizes["dom"]
    events, owned, points, width = sizes["events"], sizes["owned"], sizes["points"], sizes["width"]
    chunks = owned // CHUNK
    core = lax.axis_index("event")
    me = lax.axis_index("dom")
    odd = lax.rem(me, 2)
    step = 2 - 4 * odd
    buddy = (1 - core, me)
    partner = (core, me + 1 - 2 * odd)
    has_out = jnp.logical_and(me + step >= 0, me + step < n)
    has_in = jnp.logical_and(me - step >= 0, me - step < n)
    far_out = (core, jnp.where(has_out, me + step, me - step))
    far_in = (core, jnp.where(has_in, me - step, me + step))

    def fetch(side, c):
        start = (core if side else 1 - core) * owned + c * CHUNK
        return pltpu.make_async_copy(
            kernels.at[:, 0, pl.ds(start, CHUNK)], kbuf.at[side, c], ksem.at[side, c]
        )

    for side in (0, 1):
        for c in range(chunks):
            fetch(side, c).start()
    get_tables = pltpu.make_async_copy(tables, tab.at[pl.ds(1, sizes["tables"])], tsem.at[0])
    get_tables.start()

    barrier = pltpu.get_barrier_semaphore()
    pl.semaphore_signal(barrier, inc=1, device_id=buddy, device_id_type=MESH)
    pl.semaphore_signal(barrier, inc=1, device_id=partner, device_id_type=MESH)

    @pl.when(has_out)
    def _():
        pl.semaphore_signal(barrier, inc=1, device_id=far_out, device_id_type=MESH)

    @pl.when(has_in)
    def _():
        pl.semaphore_signal(barrier, inc=1, device_id=far_in, device_id_type=MESH)

    tab[0] = jnp.zeros((width, width), tab.dtype)
    acc[...] = jnp.zeros_like(acc)
    stage[...] = jnp.zeros_like(stage)
    vol[...] = volume[0].astype(jnp.float32)
    other = pl.multiple_of((1 - core) * owned, owned)
    own = pl.multiple_of(core * owned, owned)
    count_out[...] = sum(counts[e, 0, pl.ds(other, owned)] for e in range(events))
    pl.semaphore_wait(barrier, 2 + has_out.astype(jnp.int32) + has_in.astype(jnp.int32))

    def remote(src, dst, sems, where, device):
        return pltpu.make_async_remote_copy(
            src_ref=src, dst_ref=dst, send_sem=sems.at[(0, *where)], recv_sem=sems.at[(1, *where)],
            device_id=device, device_id_type=MESH,
        )

    send_count = remote(count_out, count_in, csem, (0,), buddy)
    send_index = remote(index_vmem, index_mate, isem, (0,), partner)
    pass_index = remote(index_mate, index_far, isem, (1,), far_out)
    send_part = lambda c: remote(part_out.at[c], part_in.at[c], xsem, (c,), buddy)
    send_source = lambda c: remote(source.at[c], mate.at[c], msem, (c,), partner)
    pass_source = lambda c: remote(mate.at[c], far.at[c], fsem, (c,), far_out)
    send_count.start()
    send_index.start()

    def event_sum(side, c, b):
        total = kbuf[side, c, 0, b].astype(jnp.float32)
        for e in range(1, events):
            total = total + kbuf[side, c, e, b].astype(jnp.float32)
        return total.astype(jnp.bfloat16)

    def give(c, carry):
        fetch(0, c).wait()
        for b in range(CHUNK):
            part_out[c, b] = event_sum(0, c, b)
        send_part(c).start()
        return carry

    lax.fori_loop(0, chunks, give, 0)

    send_count.wait()
    hits = sum(counts[e, 0, pl.ds(own, owned)] for e in range(events)) + count_in[...]
    scale[...] = vol[...] / jnp.sqrt(1.0 + hits.astype(jnp.float32))

    def weigh(c, carry):
        fetch(1, c).wait()
        send_part(c).wait_recv()
        for b in range(CHUNK):
            row = pl.ds(c * CHUNK + b, 1)
            total = event_sum(1, c, b).astype(jnp.float32) + part_in[c, b].astype(jnp.float32)
            stage[b, :points] = total * scale[row]
            stage[b, points : points + 1] = vol[row]
        for b in range(CHUNK):
            source[c, :, b * width : (b + 1) * width] = stage[b].astype(jnp.bfloat16)
        send_source(c).start()
        return carry

    lax.fori_loop(0, chunks, weigh, 0)
    get_tables.wait()

    def multiply(blocks, indices, c, shift, first, last):
        def group(g, carry):
            for h in range(CHUNK // 2):
                pair = g * (CHUNK // 2) + h
                weights = jnp.concatenate(
                    [
                        jnp.concatenate(
                            [tab[indices[c * CHUNK + b, shift + 2 * pair + t]] for t in (0, 1)],
                            axis=1,
                        )
                        for b in range(CHUNK)
                    ],
                    axis=0,
                )
                acc[pair] += jnp.dot(blocks[c], weights, preferred_element_type=jnp.float32)
            return carry

        lax.fori_loop(first, last, group, 0)

    send_index.wait()

    @pl.when(has_out)
    def _():
        pass_index.start()

    to_mate = pltpu.make_async_copy(index_mate, index_mate_s, tsem.at[1])
    to_mate.start()
    to_mate.wait()

    def far_part(c):
        pass_source(c).wait_recv()
        multiply(far, index_far_s, c, 2 * owned * (1 - odd), odd * c, jnp.where(odd == 1, chunks, c + 1))

    def work(c, carry):
        send_source(c).wait_recv()

        @pl.when(has_out)
        def _():
            pass_source(c).start()

        multiply(source, index_smem, c, owned, 0, chunks)
        multiply(mate, index_mate_s, c, 2 * owned * odd, (1 - odd) * c, jnp.where(odd == 1, c + 1, chunks))

        @pl.when(jnp.logical_and(has_in, c == 0))
        def _():
            pass_index.wait_recv()
            to_far = pltpu.make_async_copy(index_far, index_far_s, tsem.at[2])
            to_far.start()
            to_far.wait()

        @pl.when(jnp.logical_and(has_in, c >= 1))
        def _():
            far_part(c - 1)

        return carry

    lax.fori_loop(0, chunks, work, 0)

    @pl.when(has_in)
    def _():
        far_part(chunks - 1)

    def finish(i, carry):
        for t in (0, 1):
            lanes = slice(t * width, (t + 1) * width)
            inverse = 1.0 / acc[i, points : points + 1, lanes]
            out[2 * i + t] = (acc[i, :points, lanes] * inverse).astype(out.dtype)
        return carry

    lax.fori_loop(0, owned // 2, finish, 0)

    def drain(c, carry):
        send_part(c).wait_send()
        send_source(c).wait_send()

        @pl.when(has_out)
        def _():
            pass_source(c).wait_send()

        return carry

    lax.fori_loop(0, chunks, drain, 0)

    @pl.when(has_out)
    def _():
        pass_index.wait_send()


def per_device(kernels, counts, volume, tables, pair_offset, pair_table):
    events, owned = kernels.shape[0], volume.shape[1]
    points, width = kernels.shape[3:]
    rows = -(-(points + 1) // 16) * 16
    chunks = owned // CHUNK
    lanes = -(-3 * owned // 128) * 128
    targets = jnp.arange(owned, dtype=jnp.int32)[:, None] + pair_offset[0, 0]
    here = targets[:, :, None] == jnp.arange(lanes, dtype=jnp.int32)
    index = jnp.sum(jnp.where(here, pair_table[0, 0][:, :, None] + 1, 0), axis=1, dtype=jnp.int32)
    sizes = dict(
        dom=lax.axis_size("dom"), events=events, owned=owned, points=points, width=width,
        tables=tables.shape[0],
    )
    vmem = pl.BlockSpec(memory_space=pltpu.VMEM)
    hbm = pl.BlockSpec(memory_space=pl.ANY)
    dma = pltpu.SemaphoreType.DMA
    bf16, f32, i32 = jnp.bfloat16, jnp.float32, jnp.int32
    blocks = pltpu.VMEM((chunks, rows, CHUNK * width), bf16)
    return pl.pallas_call(
        functools.partial(kernel, sizes),
        out_shape=jax.ShapeDtypeStruct((owned, points, width), bf16),
        in_specs=[hbm, vmem, vmem, hbm, pl.BlockSpec(memory_space=pltpu.SMEM), vmem],
        out_specs=vmem,
        scratch_shapes=[
            pltpu.VMEM((2, chunks, events, CHUNK, points, width), bf16),
            pltpu.VMEM((chunks, CHUNK, points, width), bf16),
            pltpu.VMEM((chunks, CHUNK, points, width), bf16),
            pltpu.VMEM((owned, width), i32),
            pltpu.VMEM((owned, width), i32),
            pltpu.VMEM((owned, width), f32),
            pltpu.VMEM((owned, width), f32),
            pltpu.VMEM((CHUNK, rows, width), f32),
            blocks, blocks, blocks,
            pltpu.VMEM((tables.shape[0] + 1, width, width), bf16),
            pltpu.VMEM((owned // 2, rows, 2 * width), f32),
            pltpu.VMEM((owned, lanes), i32),
            pltpu.VMEM((owned, lanes), i32),
            pltpu.SMEM((owned, lanes), i32),
            pltpu.SMEM((owned, lanes), i32),
            dma((2, chunks)),
            dma((3,)),
            dma((2, 1)),
            dma((2, chunks)),
            dma((2, 2)),
            dma((2, chunks)),
            dma((2, chunks)),
        ],
        compiler_params=pltpu.CompilerParams(
            collective_id=0, has_side_effects=True, vmem_limit_bytes=40 * 2**20
        ),
    )(kernels, counts, volume, tables, index, index)[None]


def solution(mesh):
    in_specs = (
        P("event", "dom", None, None, None),
        P("event", "dom", None, None),
        P("dom", "event", None),
        P(),
        P("dom", "event", None, None),
        P("dom", "event", None, None),
    )
    out_specs = P("dom", "event", None, None)
    return jax.shard_map(
        per_device, mesh=mesh, in_specs=in_specs, out_specs=out_specs, check_vma=False
    )
```

```python
import functools

import jax
import jax.numpy as jnp
from jax import lax
from jax.experimental import pallas as pl
from jax.experimental.pallas import tpu as pltpu
from jax.sharding import PartitionSpec as P

UNIT = 2
CHUNK = 8
HALF = 16
MESH = pl.DeviceIdType.MESH


def kernel(
    sizes,
    kernels, counts, volume, tables, index_smem, index_vmem, out,
    kbuf, part_out, part_in, count_out, count_in, stage, result,
    source, mate, far, tab, acc, index_mate, index_far, index_mate_s, index_far_s,
    ksem, tsem, csem, xsem, isem, msem, fsem,
):
    n = sizes["dom"]
    events, owned, points, width = sizes["events"], sizes["owned"], sizes["points"], sizes["width"]
    cut = sizes["cut"]
    rows = stage.shape[0] // HALF
    slabs, halves, units, chunks = points // cut, owned // HALF, owned // UNIT, owned // CHUNK
    core = lax.axis_index("event")
    me = lax.axis_index("dom")
    odd = lax.rem(me, 2)
    step = 2 - 4 * odd
    buddy = (1 - core, me)
    partner = (core, me + 1 - 2 * odd)
    has_out = jnp.logical_and(me + step >= 0, me + step < n)
    has_in = jnp.logical_and(me - step >= 0, me - step < n)
    far_out = (core, jnp.where(has_out, me + step, me - step))
    far_in = (core, jnp.where(has_in, me - step, me + step))

    def fetch(side, h):
        start = pl.multiple_of((core if side else 1 - core) * owned + h * HALF, HALF)
        return pltpu.make_async_copy(
            kernels.at[:, 0, :, pl.ds(start, HALF)], kbuf.at[side, h], ksem.at[side, h]
        )

    for h in range(halves):
        for side in (0, 1):
            fetch(side, h).start()
    get_tables = pltpu.make_async_copy(tables, tab.at[pl.ds(1, sizes["tables"])], tsem.at[0])
    get_tables.start()

    barrier = pltpu.get_barrier_semaphore()
    pl.semaphore_signal(barrier, inc=1, device_id=buddy, device_id_type=MESH)
    pl.semaphore_signal(barrier, inc=1, device_id=partner, device_id_type=MESH)

    @pl.when(has_out)
    def _():
        pl.semaphore_signal(barrier, inc=1, device_id=far_out, device_id_type=MESH)

    @pl.when(has_in)
    def _():
        pl.semaphore_signal(barrier, inc=1, device_id=far_in, device_id_type=MESH)

    tab[0] = jnp.zeros((width, width), tab.dtype)
    acc[...] = jnp.zeros_like(acc)
    stage[(points + 1) * HALF :] = jnp.zeros((stage.shape[0] - (points + 1) * HALF, width), jnp.float32)
    vol = volume[0].astype(jnp.float32)
    other = pl.multiple_of((1 - core) * owned, owned)
    own = pl.multiple_of(core * owned, owned)
    count_out[...] = sum(counts[e, 0, pl.ds(other, owned)] for e in range(events))
    pl.semaphore_wait(barrier, 2 + has_out.astype(jnp.int32) + has_in.astype(jnp.int32))

    def remote(src, dst, sems, where, device):
        return pltpu.make_async_remote_copy(
            src_ref=src, dst_ref=dst, send_sem=sems.at[(0, *where)], recv_sem=sems.at[(1, *where)],
            device_id=device, device_id_type=MESH,
        )

    send_count = remote(count_out, count_in, csem, (0,), buddy)
    send_index = remote(index_vmem, index_mate, isem, (0,), partner)
    pass_index = remote(index_mate, index_far, isem, (1,), far_out)
    send_part = lambda h, q: remote(part_out.at[h, q], part_in.at[h, q], xsem, (h, q), buddy)
    send_source = lambda u: remote(source.at[u], mate.at[u], msem, (u,), partner)
    pass_source = lambda u: remote(mate.at[u], far.at[u], fsem, (u,), far_out)
    send_count.start()
    send_index.start()

    def event_sum(side, h, g):
        total = kbuf[side, h, 0, g].astype(jnp.float32)
        for e in range(1, events):
            total = total + kbuf[side, h, e, g].astype(jnp.float32)
        return total.astype(jnp.bfloat16)

    for h in range(halves):
        fetch(0, h).wait()

        def give(q, carry):
            for r in range(cut):
                part_out[h, q, r] = event_sum(0, h, q * cut + r)
            send_part(h, q).start()
            return carry

        lax.fori_loop(0, slabs, give, 0)

    send_count.wait()
    hits = sum(counts[e, 0, pl.ds(own, owned)] for e in range(events)) + count_in[...]
    scale = vol / jnp.sqrt(1.0 + hits.astype(jnp.float32))

    for h in range(halves):
        fetch(1, h).wait()
        here = slice(h * HALF, (h + 1) * HALF)
        factor = scale[here]

        def weigh(q, carry):
            send_part(h, q).wait_recv()
            for r in range(cut):
                g = q * cut + r
                total = event_sum(1, h, g).astype(jnp.float32) + part_in[h, q, r].astype(jnp.float32)
                stage[pl.ds(pl.multiple_of(g * HALF, HALF), HALF)] = total * factor
            return carry

        lax.fori_loop(0, slabs, weigh, 0)
        stage[points * HALF : (points + 1) * HALF] = vol[here]
        for u in range(HALF // UNIT):
            unit = h * (HALF // UNIT) + u
            for b in range(UNIT):
                block = stage[pl.ds(u * UNIT + b, rows, stride=HALF)]
                source[unit, :, b * width : (b + 1) * width] = block.astype(jnp.bfloat16)
            send_source(unit).start()

    get_tables.wait()

    def multiply(blocks, indices, c, shift, first, last):
        left = jnp.concatenate([blocks[c * (CHUNK // UNIT) + u] for u in range(CHUNK // UNIT)], axis=1)

        def group(g, carry):
            for h in range(CHUNK // 2):
                pair = g * (CHUNK // 2) + h
                weights = jnp.concatenate(
                    [
                        jnp.concatenate(
                            [tab[indices[shift + 2 * pair + t, c * CHUNK + b]] for t in (0, 1)],
                            axis=1,
                        )
                        for b in range(CHUNK)
                    ],
                    axis=0,
                )
                acc[pair] += jnp.dot(left, weights, preferred_element_type=jnp.float32)
            return carry

        lax.fori_loop(first, last, group, 0)

    send_index.wait()

    @pl.when(has_out)
    def _():
        pass_index.start()

    to_mate = pltpu.make_async_copy(index_mate, index_mate_s, tsem.at[1])
    to_mate.start()
    to_mate.wait()

    per = CHUNK // UNIT

    def far_part(c):
        for u in range(per):
            pass_source(c * per + u).wait_recv()
        multiply(far, index_far_s, c, 2 * owned * (1 - odd), odd * c, jnp.where(odd == 1, chunks, c + 1))

    def relay(u):
        send_source(u).wait_recv()

        @pl.when(has_out)
        def _():
            pass_source(u).start()

    def work(c, carry):
        for u in range(per // 2):
            relay(c * per + u)
        multiply(source, index_smem, c, owned, 0, chunks)
        for u in range(per // 2, per):
            relay(c * per + u)
        multiply(mate, index_mate_s, c, 2 * owned * odd, (1 - odd) * c, jnp.where(odd == 1, c + 1, chunks))

        @pl.when(jnp.logical_and(has_in, c == 0))
        def _():
            pass_index.wait_recv()
            to_far = pltpu.make_async_copy(index_far, index_far_s, tsem.at[2])
            to_far.start()
            to_far.wait()

        @pl.when(jnp.logical_and(has_in, c >= 1))
        def _():
            far_part(c - 1)

        return carry

    lax.fori_loop(0, chunks, work, 0)

    @pl.when(has_in)
    def _():
        far_part(chunks - 1)

    def finish(i, carry):
        for t in (0, 1):
            lanes = slice(t * width, (t + 1) * width)
            inverse = 1.0 / acc[i, points : points + 1, lanes]
            result[pl.ds(2 * i + t, rows, stride=owned)] = acc[i, :, lanes] * inverse
        return carry

    lax.fori_loop(0, owned // 2, finish, 0)

    def write(q, carry):
        for r in range(cut):
            g = q * cut + r
            out[g] = result[pl.ds(pl.multiple_of(g * owned, owned), owned)].astype(out.dtype)
        return carry

    lax.fori_loop(0, slabs, write, 0)
    for h in range(halves):
        for q in range(slabs):
            send_part(h, q).wait_send()

    def drain(u, carry):
        send_source(u).wait_send()

        @pl.when(has_out)
        def _():
            pass_source(u).wait_send()

        return carry

    lax.fori_loop(0, units, drain, 0)

    @pl.when(has_out)
    def _():
        pass_index.wait_send()


def per_device(kernels, counts, volume, tables, pair_offset, pair_table):
    events, owned = kernels.shape[0], volume.shape[1]
    points, width = kernels.shape[3:]
    rows = -(-(points + 1) // 16) * 16
    cut = points // 5 if points % 5 == 0 else points
    units = owned // UNIT
    targets = pair_offset[0, 0].T + jnp.arange(owned, dtype=jnp.int32)
    here = targets[:, None, :] == jnp.arange(3 * owned, dtype=jnp.int32)[:, None]
    index = jnp.sum(jnp.where(here, pair_table[0, 0].T[:, None, :] + 1, 0), axis=0, dtype=jnp.int32)
    index = jnp.pad(index, ((0, 0), (0, -owned % 128)))
    sizes = dict(
        dom=lax.axis_size("dom"), events=events, owned=owned, points=points, width=width,
        tables=tables.shape[0], cut=cut,
    )
    vmem = pl.BlockSpec(memory_space=pltpu.VMEM)
    hbm = pl.BlockSpec(memory_space=pl.ANY)
    dma = pltpu.SemaphoreType.DMA
    bf16, f32, i32 = jnp.bfloat16, jnp.float32, jnp.int32
    blocks = pltpu.VMEM((units, rows, UNIT * width), bf16)
    part = pltpu.VMEM((owned // HALF, points // cut, cut, HALF, width), bf16)
    pairs = (3 * owned, index.shape[1])
    result = pl.pallas_call(
        functools.partial(kernel, sizes),
        out_shape=jax.ShapeDtypeStruct((points, owned, width), bf16),
        in_specs=[hbm, vmem, vmem, hbm, pl.BlockSpec(memory_space=pltpu.SMEM), vmem],
        out_specs=vmem,
        scratch_shapes=[
            pltpu.VMEM((2, owned // HALF, events, points, HALF, width), bf16),
            part, part,
            pltpu.VMEM((owned, width), i32),
            pltpu.VMEM((owned, width), i32),
            pltpu.VMEM((rows * HALF, width), f32),
            pltpu.VMEM((rows * owned, width), f32),
            blocks, blocks, blocks,
            pltpu.VMEM((tables.shape[0] + 1, width, width), bf16),
            pltpu.VMEM((owned // 2, rows, 2 * width), f32),
            pltpu.VMEM(pairs, i32),
            pltpu.VMEM(pairs, i32),
            pltpu.SMEM(pairs, i32),
            pltpu.SMEM(pairs, i32),
            dma((2, owned // HALF)),
            dma((3,)),
            dma((2, 1)),
            dma((2, owned // HALF, points // cut)),
            dma((2, 2)),
            dma((2, units)),
            dma((2, units)),
        ],
        compiler_params=pltpu.CompilerParams(
            collective_id=0, has_side_effects=True, vmem_limit_bytes=60 * 2**20
        ),
    )(kernels.transpose(0, 1, 3, 2, 4), counts, volume, tables, index, index)
    return result.transpose(1, 0, 2)[None]


def solution(mesh):
    in_specs = (
        P("event", "dom", None, None, None),
        P("event", "dom", None, None),
        P("dom", "event", None),
        P(),
        P("dom", "event", None, None),
        P("dom", "event", None, None),
    )
    out_specs = P("dom", "event", None, None)
    return jax.shard_map(
        per_device, mesh=mesh, in_specs=in_specs, out_specs=out_specs, check_vma=False
    )
```

```python
import functools

import jax
import jax.numpy as jnp
from jax import lax
from jax.experimental import pallas as pl
from jax.experimental.pallas import tpu as pltpu
from jax.sharding import PartitionSpec as P

UNIT = 2
CHUNK = 8
HALF = 16
MESH = pl.DeviceIdType.MESH


def kernel(
    sizes,
    kernels, counts, volume, tables, offsets, names, out,
    kbuf, part_out, part_in, count_out, count_in, stage, result,
    source, mate, far, tab, acc, index_own, index_smem, index_mate, index_far, index_mate_s, index_far_s,
    ksem, tsem, csem, xsem, isem, msem, fsem,
):
    n = sizes["dom"]
    events, owned, points, width = sizes["events"], sizes["owned"], sizes["points"], sizes["width"]
    cut = sizes["cut"]
    rows = stage.shape[0] // HALF
    slabs, halves, units, chunks = points // cut, owned // HALF, owned // UNIT, owned // CHUNK
    core = lax.axis_index("event")
    me = lax.axis_index("dom")
    odd = lax.rem(me, 2)
    step = 2 - 4 * odd
    buddy = (1 - core, me)
    partner = (core, me + 1 - 2 * odd)
    has_out = jnp.logical_and(me + step >= 0, me + step < n)
    has_in = jnp.logical_and(me - step >= 0, me - step < n)
    far_out = (core, jnp.where(has_out, me + step, me - step))
    far_in = (core, jnp.where(has_in, me - step, me + step))

    def fetch(side, h):
        start = pl.multiple_of((core if side else 1 - core) * owned + h * HALF, HALF)
        return pltpu.make_async_copy(
            kernels.at[:, 0, :, pl.ds(start, HALF)], kbuf.at[side, h], ksem.at[side, h]
        )

    for h in range(halves):
        for side in (0, 1):
            fetch(side, h).start()
    get_tables = pltpu.make_async_copy(tables, tab.at[pl.ds(1, sizes["tables"])], tsem.at[0])
    get_tables.start()

    group = width // owned
    spread = lambda value: jnp.concatenate([value] * group, axis=1)
    targets = spread(offsets[...] + lax.broadcasted_iota(jnp.int32, offsets.shape, 1))
    found = spread(names[...] + 1)
    places = lax.broadcasted_iota(jnp.int32, index_own.shape, 0) * group
    places = places + lax.broadcasted_iota(jnp.int32, index_own.shape, 1) // owned
    index = jnp.zeros(index_own.shape, jnp.int32)
    for k in range(offsets.shape[0]):
        index = jnp.where(targets[k : k + 1] == places, found[k : k + 1], index)
    index_own[...] = index
    third = owned // group

    barrier = pltpu.get_barrier_semaphore()
    pl.semaphore_signal(barrier, inc=1, device_id=buddy, device_id_type=MESH)
    pl.semaphore_signal(barrier, inc=1, device_id=partner, device_id_type=MESH)

    @pl.when(has_out)
    def _():
        pl.semaphore_signal(barrier, inc=1, device_id=far_out, device_id_type=MESH)

    @pl.when(has_in)
    def _():
        pl.semaphore_signal(barrier, inc=1, device_id=far_in, device_id_type=MESH)

    tab[0] = jnp.zeros((width, width), tab.dtype)
    acc[...] = jnp.zeros_like(acc)
    stage[(points + 1) * HALF :] = jnp.zeros((stage.shape[0] - (points + 1) * HALF, width), jnp.float32)
    vol = volume[0].astype(jnp.float32)
    other = pl.multiple_of((1 - core) * owned, owned)
    own = pl.multiple_of(core * owned, owned)
    count_out[...] = sum(counts[e, 0, pl.ds(other, owned)] for e in range(events))
    pl.semaphore_wait(barrier, 2 + has_out.astype(jnp.int32) + has_in.astype(jnp.int32))

    def remote(src, dst, sems, where, device):
        return pltpu.make_async_remote_copy(
            src_ref=src, dst_ref=dst, send_sem=sems.at[(0, *where)], recv_sem=sems.at[(1, *where)],
            device_id=device, device_id_type=MESH,
        )

    send_count = remote(count_out, count_in, csem, (0,), buddy)
    send_index = remote(index_own, index_mate, isem, (0,), partner)
    pass_index = remote(index_mate, index_far, isem, (1,), far_out)
    send_part = lambda h, q: remote(part_out.at[h, q], part_in.at[h, q], xsem, (h, q), buddy)
    send_source = lambda u: remote(source.at[u], mate.at[u], msem, (u,), partner)
    pass_source = lambda u: remote(mate.at[u], far.at[u], fsem, (u,), far_out)
    send_count.start()
    to_own = pltpu.make_async_copy(index_own.at[pl.ds(third, third)], index_smem, tsem.at[3])
    to_own.start()
    send_index.start()

    def event_sum(side, h, g):
        total = kbuf[side, h, 0, g].astype(jnp.float32)
        for e in range(1, events):
            total = total + kbuf[side, h, e, g].astype(jnp.float32)
        return total.astype(jnp.bfloat16)

    for h in range(halves):
        fetch(0, h).wait()

        def give(q, carry):
            for r in range(cut):
                part_out[h, q, r] = event_sum(0, h, q * cut + r)
            send_part(h, q).start()
            return carry

        lax.fori_loop(0, slabs, give, 0)

    send_count.wait()
    hits = sum(counts[e, 0, pl.ds(own, owned)] for e in range(events)) + count_in[...]
    scale = vol / jnp.sqrt(1.0 + hits.astype(jnp.float32))

    for h in range(halves):
        fetch(1, h).wait()
        here = slice(h * HALF, (h + 1) * HALF)
        factor = scale[here]

        def weigh(q, carry):
            send_part(h, q).wait_recv()
            for r in range(cut):
                g = q * cut + r
                total = event_sum(1, h, g).astype(jnp.float32) + part_in[h, q, r].astype(jnp.float32)
                stage[pl.ds(pl.multiple_of(g * HALF, HALF), HALF)] = total * factor
            return carry

        lax.fori_loop(0, slabs, weigh, 0)
        stage[points * HALF : (points + 1) * HALF] = vol[here]
        for u in range(HALF // UNIT):
            unit = h * (HALF // UNIT) + u
            for b in range(UNIT):
                block = stage[pl.ds(u * UNIT + b, rows, stride=HALF)]
                source[unit, :, b * width : (b + 1) * width] = block.astype(jnp.bfloat16)
            send_source(unit).start()

    get_tables.wait()
    to_own.wait()

    def multiply(blocks, indices, c, first, last):
        left = jnp.concatenate([blocks[c * (CHUNK // UNIT) + u] for u in range(CHUNK // UNIT)], axis=1)

        def name(g, at, b):
            return indices[g * (CHUNK // group) + at // group, at % group * owned + c * CHUNK + b]

        def targets_of(g, carry):
            for h in range(CHUNK // 2):
                pair = g * (CHUNK // 2) + h
                weights = jnp.concatenate(
                    [
                        jnp.concatenate(
                            [tab[name(g, 2 * h + t, b)] for t in (0, 1)], axis=1
                        )
                        for b in range(CHUNK)
                    ],
                    axis=0,
                )
                acc[pair] += jnp.dot(left, weights, preferred_element_type=jnp.float32)
            return carry

        lax.fori_loop(first, last, targets_of, 0)

    send_index.wait()

    @pl.when(has_out)
    def _():
        pass_index.start()

    to_mate = pltpu.make_async_copy(
        index_mate.at[pl.ds(pl.multiple_of(2 * third * odd, third), third)], index_mate_s, tsem.at[1]
    )
    to_mate.start()
    to_mate.wait()

    per = CHUNK // UNIT

    def far_part(c):
        for u in range(per):
            pass_source(c * per + u).wait_recv()
        multiply(far, index_far_s, c, odd * c, jnp.where(odd == 1, chunks, c + 1))

    def relay(u):
        send_source(u).wait_recv()

        @pl.when(has_out)
        def _():
            pass_source(u).start()

    def work(c, carry):
        for u in range(per // 2):
            relay(c * per + u)
        multiply(source, index_smem, c, 0, chunks)
        for u in range(per // 2, per):
            relay(c * per + u)
        multiply(mate, index_mate_s, c, (1 - odd) * c, jnp.where(odd == 1, c + 1, chunks))

        @pl.when(jnp.logical_and(has_in, c == 0))
        def _():
            pass_index.wait_recv()
            to_far = pltpu.make_async_copy(
                index_far.at[pl.ds(pl.multiple_of(2 * third * (1 - odd), third), third)],
                index_far_s, tsem.at[2],
            )
            to_far.start()
            to_far.wait()

        @pl.when(jnp.logical_and(has_in, c >= 1))
        def _():
            far_part(c - 1)

        return carry

    lax.fori_loop(0, chunks, work, 0)

    @pl.when(has_in)
    def _():
        far_part(chunks - 1)

    def finish(i, carry):
        for t in (0, 1):
            lanes = slice(t * width, (t + 1) * width)
            inverse = 1.0 / acc[i, points : points + 1, lanes]
            result[pl.ds(2 * i + t, rows, stride=owned)] = acc[i, :, lanes] * inverse
        return carry

    lax.fori_loop(0, owned // 2, finish, 0)

    def write(q, carry):
        for r in range(cut):
            g = q * cut + r
            out[g] = result[pl.ds(pl.multiple_of(g * owned, owned), owned)].astype(out.dtype)
        return carry

    lax.fori_loop(0, slabs, write, 0)
    for h in range(halves):
        for q in range(slabs):
            send_part(h, q).wait_send()

    def drain(u, carry):
        send_source(u).wait_send()

        @pl.when(has_out)
        def _():
            pass_source(u).wait_send()

        return carry

    lax.fori_loop(0, units, drain, 0)

    @pl.when(has_out)
    def _():
        pass_index.wait_send()


def per_device(kernels, counts, volume, tables, pair_offset, pair_table):
    events, owned = kernels.shape[0], volume.shape[1]
    points, width = kernels.shape[3:]
    rows = -(-(points + 1) // 16) * 16
    cut = points // 5 if points % 5 == 0 else points
    units = owned // UNIT
    sizes = dict(
        dom=lax.axis_size("dom"), events=events, owned=owned, points=points, width=width,
        tables=tables.shape[0], cut=cut,
    )
    vmem = pl.BlockSpec(memory_space=pltpu.VMEM)
    hbm = pl.BlockSpec(memory_space=pl.ANY)
    dma = pltpu.SemaphoreType.DMA
    bf16, f32, i32 = jnp.bfloat16, jnp.float32, jnp.int32
    blocks = pltpu.VMEM((units, rows, UNIT * width), bf16)
    part = pltpu.VMEM((owned // HALF, points // cut, cut, HALF, width), bf16)
    pairs = (3 * owned * owned // width, width)
    third = pltpu.SMEM((owned * owned // width, width), i32)
    result = pl.pallas_call(
        functools.partial(kernel, sizes),
        out_shape=jax.ShapeDtypeStruct((points, owned, width), bf16),
        in_specs=[hbm, vmem, vmem, hbm, vmem, vmem],
        out_specs=vmem,
        scratch_shapes=[
            pltpu.VMEM((2, owned // HALF, events, points, HALF, width), bf16),
            part, part,
            pltpu.VMEM((owned, width), i32),
            pltpu.VMEM((owned, width), i32),
            pltpu.VMEM((rows * HALF, width), f32),
            pltpu.VMEM((rows * owned, width), f32),
            blocks, blocks, blocks,
            pltpu.VMEM((tables.shape[0] + 1, width, width), bf16),
            pltpu.VMEM((owned // 2, rows, 2 * width), f32),
            pltpu.VMEM(pairs, i32),
            third,
            pltpu.VMEM(pairs, i32),
            pltpu.VMEM(pairs, i32),
            third,
            third,
            dma((2, owned // HALF)),
            dma((4,)),
            dma((2, 1)),
            dma((2, owned // HALF, points // cut)),
            dma((2, 2)),
            dma((2, units)),
            dma((2, units)),
        ],
        compiler_params=pltpu.CompilerParams(
            collective_id=0, has_side_effects=True, vmem_limit_bytes=60 * 2**20
        ),
    )(kernels.transpose(0, 1, 3, 2, 4), counts, volume, tables, pair_offset[0, 0].T, pair_table[0, 0].T)
    return result.transpose(1, 0, 2)[None]


def solution(mesh):
    in_specs = (
        P("event", "dom", None, None, None),
        P("event", "dom", None, None),
        P("dom", "event", None),
        P(),
        P("dom", "event", None, None),
        P("dom", "event", None, None),
    )
    out_specs = P("dom", "event", None, None)
    return jax.shard_map(
        per_device, mesh=mesh, in_specs=in_specs, out_specs=out_specs, check_vma=False
    )
```
